32 devices in a mesh: grp: 2 (over x), blk: 16 (over z, y, core).
Axes of the slice: x: 2, y: 2, z: 4, core: 2. Of those that a mesh axis runs over, the one named last changes fastest.
Arguments:
- slab: bfloat16 [64, 4, 1, 2, 256, 256], P(('grp', 'blk')), parts along dimension 0, may hold values from -6 to 6
- slab_cols: int32 [32, 4], P('blk'), may hold values from 0 to 31, as said below
- panels: bfloat16 [64, 4, 1, 2, 256, 256], P(('grp', 'blk')), parts along dimension 0, may hold values from -0.25 to 0.25
- panel_rows: int32 [32, 4], P('blk'), may hold values from 0 to 31, as said below
- panel_live: int32 [32], P('blk'), may hold values from 1 to 4, as said below
Outputs:
- multiples: bfloat16 [64, 1, 2, 256, 2560], P(('grp', 'blk')), parts along dimension 0
The draws below stay inside these ranges and needn't reach their ends.
There are 2 independent parts, one for each index of `grp`. The reference program is written for one: setup_inputs(seed, part) draws one part's arguments, and reference() takes and returns one part's arrays. A program takes and returns all parts, laid end to end along the dimension named above; an argument that names none is the same for every part. Nothing has to cross between parts.
Inputs may be any that keep to these rules, and one draw needn't show every extreme that they name: `slab_cols`: within a row panel r the entries are distinct, each within cycle distance 4 (modulo 32) of 2 * (r // 2) + 1. `panel_rows`: within a column panel c the entries are distinct, each within cycle distance 4 (modulo 32) of 2 * (c // 2) + 1; slots from panel_live[c] on hold no data. `panel_live`: some column panel has all 4 slots live.
All inputs are finite; a program needn't handle non-finite values.
Results may differ from the reference program's by a relative error of at most 0.001.
Values may be sent and summed in bfloat16 or wider, within the bound.
No kernel may reach another device: no remote copies, remote signals or barrier semaphores. Data moves between devices by JAX's collectives and lax.ppermute only.
A program may use at most 128 MiB of HBM per device.

```python
import jax
import jax.numpy as jnp
from jax import lax

BLOCK = 256
FREQS = 1
SLAB_LIVE = 4
PANEL_LIVE = 4
ROWS_DEV = 2
COLS_DEV = 2
HALF = 2
KB_DEV = 2
SPREAD = 4
ROWPANELS = 32
COLPANELS = 32
KBLOCKS = 32
N_BLK = 16


def local_lists(key, list_count, centres, spread, kept_count, modulus):
    key_list = jax.random.split(key, list_count)
    chosen_offsets = jax.vmap(lambda single: jax.random.permutation(single, 2 * spread + 1)[:kept_count])(key_list)
    return ((centres[:, None] + chosen_offsets.astype(jnp.int32) - spread) % modulus).astype(jnp.int32)


def draw_slab_cols(key, part):
    key = jax.random.fold_in(key, 11)
    centres = jnp.arange(ROWPANELS, dtype=jnp.int32) // ROWS_DEV * KB_DEV + KB_DEV // 2
    return local_lists(key, ROWPANELS, centres, SPREAD, SLAB_LIVE, KBLOCKS)


def draw_panel_rows(key, part):
    key = jax.random.fold_in(key, 12)
    centres = jnp.arange(COLPANELS, dtype=jnp.int32) // COLS_DEV * KB_DEV + KB_DEV // 2
    return local_lists(key, COLPANELS, centres, SPREAD, PANEL_LIVE, KBLOCKS)


def draw_panel_live(key, part):
    key = jax.random.fold_in(key, 13)
    first_key, second_key = jax.random.split(key)
    counts_drawn = jax.random.randint(first_key, (COLPANELS,), 1, PANEL_LIVE + 1, dtype=jnp.int32)
    fullest = jax.random.randint(second_key, (), 0, COLPANELS, dtype=jnp.int32)
    positions = jnp.arange(COLPANELS, dtype=jnp.int32)
    return jnp.where(positions == fullest, PANEL_LIVE, counts_drawn).astype(jnp.int32)


def block_levels(rng, extent, cuts, smallest, high):
    factor_of = 1.0
    for position, blocks in cuts:
        heights = jax.random.uniform(jax.random.fold_in(jax.random.fold_in(rng, 6), position), (blocks,), jnp.float32, smallest / len(cuts), high / len(cuts))
        factor_of = factor_of * jnp.repeat(jnp.exp(heights), extent[position] // blocks).reshape((-1,) + (1,) * (len(extent) - 1 - position))
    return factor_of


def noise(stream_key, extent, deviation, reach, cuts=(), kind=jnp.bfloat16):
    factor_of = block_levels(stream_key, extent, cuts, -0.22, 0.18) if cuts else 1.0
    result = jax.random.normal(stream_key, extent, jnp.float32) * deviation * factor_of
    return jnp.minimum(jnp.maximum(result, -reach), reach).astype(kind)


def setup_inputs(seed: int = 0, part: int = 0) -> dict:
    splits = jax.random.split(jax.random.key(seed), 6)
    part_splits = jax.random.split(jax.random.fold_in(splits[5], part), 6)
    slab = noise(part_splits[0], (ROWPANELS, SLAB_LIVE, FREQS, 2, BLOCK, BLOCK), 1.0, 6.0, ((0, 16),))
    slab_cols = draw_slab_cols(jax.random.fold_in(splits[5], 71), part)
    panels = noise(part_splits[2], (COLPANELS, PANEL_LIVE, FREQS, 2, BLOCK, BLOCK), (2 * BLOCK) ** -0.5, 0.25, ((0, 16),))
    panel_rows = draw_panel_rows(jax.random.fold_in(splits[5], 71), part)
    panel_live = draw_panel_live(jax.random.fold_in(splits[5], 71), part)
    return dict(slab=slab, slab_cols=slab_cols, panels=panels, panel_rows=panel_rows, panel_live=panel_live)


def reference(slab, slab_cols, panels, panel_rows, panel_live):
    slot_ids = jnp.arange(PANEL_LIVE, dtype=jnp.int32)
    live_slots = slot_ids[None, :] < panel_live[:, None]
    reach_offsets = jnp.arange(-HALF, HALF + 1, dtype=jnp.int32)
    within = jnp.arange(COLS_DEV, dtype=jnp.int32)

    def one_panel(row_panel):
        owners = (row_panel // ROWS_DEV + reach_offsets) % N_BLK
        chosen = (owners[:, None] * COLS_DEV + within[None, :]).reshape(-1).astype(jnp.int32)
        gathered = panels[chosen].astype(jnp.float32)
        index_rows = panel_rows[chosen]
        usable = live_slots[chosen]
        own_index = slab_cols[row_panel]
        matches = ((index_rows[:, :, None] == own_index[None, None, :]) & usable[:, :, None]).astype(jnp.float32)
        own_blocks = slab[row_panel].astype(jnp.float32)
        lifted = jnp.einsum("cji,ifpax->cjfpax", matches, own_blocks, precision=lax.Precision.HIGHEST)
        real_part = lifted[:, :, :, 0]
        imag_part = lifted[:, :, :, 1]
        panel_real = gathered[:, :, :, 0]
        panel_imag = gathered[:, :, :, 1]
        form = "cjfax,cjfxb->facb"
        highest = lax.Precision.HIGHEST
        out_real = jnp.einsum(form, real_part, panel_real, precision=highest) - jnp.einsum(form, imag_part, panel_imag, precision=highest)
        out_imag = jnp.einsum(form, real_part, panel_imag, precision=highest) + jnp.einsum(form, imag_part, panel_real, precision=highest)
        combined = jnp.stack([out_real, out_imag], 1)
        return combined.reshape(FREQS, 2, BLOCK, -1).astype(jnp.bfloat16)

    return lax.map(one_panel, jnp.arange(ROWPANELS, dtype=jnp.int32))
```

```python
import functools

import jax
import jax.numpy as jnp
from jax import lax
from jax.experimental import pallas as pl
from jax.experimental.pallas import tpu as pltpu
from jax.sharding import PartitionSpec as P

HALF = 2
CHUNKS = (2, 2, 2, 2)


def product_kernel(groups, arrays, slots, aliased, *refs):
    match_ref, place_ref, slab_ref = refs[:3]
    chunk_refs = refs[3 : 3 + arrays]
    refs = refs[3 + arrays + aliased :]
    out_ref, slab_v, block_v, total, out_v, slab_sem, block_sem, out_sem = refs
    rows, _, freqs = slab_ref.shape[:3]
    side = slab_ref.shape[4]
    sources = [ref.at[i] for ref in chunk_refs for i in range(ref.shape[0])]

    def needed(b):
        hit = match_ref[b * rows] >= 0
        for r in range(1, rows):
            hit = jnp.logical_or(hit, match_ref[b * rows + r] >= 0)
        return hit

    slab_copy = pltpu.make_async_copy(slab_ref, slab_v, slab_sem)
    slab_copy.start()
    for b, source in enumerate(sources):

        @pl.when(needed(b))
        def _():
            pltpu.make_async_copy(source, block_v.at[b], block_sem.at[b]).start()

    slab_copy.wait()

    def out_copy(g, r):
        return pltpu.make_async_copy(
            out_v.at[g, r],
            out_ref.at[r, :, :, :, pl.ds(pl.multiple_of(place_ref[g] * side, side), side)],
            out_sem.at[g, r],
        )

    def group(g, carry):
        total[...] = jnp.zeros_like(total)

        def slot(j, carry):
            b = g * slots + j

            @pl.when(needed(b))
            def _():
                pltpu.make_async_copy(block_v.at[b], block_v.at[b], block_sem.at[b]).wait()

            for r in range(rows):
                own = match_ref[b * rows + r]

                @pl.when(own >= 0)
                def _():
                    dot = functools.partial(jnp.dot, preferred_element_type=jnp.float32)
                    for f in range(freqs):
                        real, imag = slab_v[r, own, f, 0], slab_v[r, own, f, 1]
                        b_real, b_imag = block_v[b, f, 0], block_v[b, f, 1]
                        total[r, f, 0] += dot(real, b_real) - dot(imag, b_imag)
                        total[r, f, 1] += dot(real, b_imag) + dot(imag, b_real)

            return carry

        lax.fori_loop(0, slots, slot, 0)
        for r in range(rows):
            out_v[g, r] = total[r].astype(out_v.dtype)
            out_copy(g, r).start()
        return carry

    lax.fori_loop(0, groups, group, 0)

    def drain(g, carry):
        for r in range(rows):
            out_copy(g, r).wait()
        return carry

    lax.fori_loop(0, groups, drain, 0)


def products(slab, match, place, chunks, out_shape, before=None):
    rows, _, freqs, parts, side, _ = slab.shape
    groups = place.shape[0]
    slots = sum(chunk.shape[0] for chunk in chunks) // groups
    any_spec = pl.BlockSpec(memory_space=pl.ANY)
    smem_spec = pl.BlockSpec(memory_space=pltpu.SMEM)
    operands = [match, place, slab, *chunks] + ([] if before is None else [before])
    return pl.pallas_call(
        functools.partial(product_kernel, groups, len(chunks), slots, before is not None),
        out_shape=out_shape,
        in_specs=[smem_spec, smem_spec] + [any_spec] * (len(operands) - 2),
        out_specs=any_spec,
        scratch_shapes=[
            pltpu.VMEM(slab.shape, slab.dtype),
            pltpu.VMEM((groups * slots, freqs, parts, side, side), slab.dtype),
            pltpu.VMEM((rows, freqs, parts, side, side), jnp.float32),
            pltpu.VMEM((groups, rows, freqs, parts, side, side), out_shape.dtype),
            pltpu.SemaphoreType.DMA,
            pltpu.SemaphoreType.DMA((groups * slots,)),
            pltpu.SemaphoreType.DMA((groups, rows)),
        ],
        input_output_aliases={} if before is None else {len(operands) - 1: 0},
        compiler_params=pltpu.CompilerParams(vmem_limit_bytes=32 * 2**20),
        cost_estimate=pl.CostEstimate(
            flops=groups * slots * rows * 4 * freqs * side**3,
            bytes_accessed=2 * (slab.size + groups * (slots + rows) * freqs * parts * side * side),
            transcendentals=0,
        ),
    )(*operands)


def shards(slab, slab_cols, panels, panel_rows, panel_live):
    rows, _, freqs, parts, side, _ = slab.shape
    cols, slots = panel_rows.shape
    devices = lax.axis_size("blk")
    me = lax.axis_index("blk")
    core, odd = me % 2, (me // 2) % 2

    def permuted(value, target):
        return lax.ppermute(value, "blk", [(i, target(i)) for i in range(devices)])

    def partner_chip(i):
        return i ^ 2

    def partner_core(i):
        return i ^ 1

    def onward(i):
        return (i + 4 if (i // 2) % 2 == 0 else i - 4) % devices

    live = jnp.arange(slots, dtype=jnp.int32)[None, :] < panel_live[:, None]
    own_rows = jnp.where(live, panel_rows, -1)

    blocks = panels.reshape((cols * slots,) + panels.shape[2:])
    edges = [sum(CHUNKS[:k]) for k in range(len(CHUNKS) + 1)]
    pieces = [blocks[a:b] for a, b in zip(edges[:-1], edges[1:])]
    across, along, passed = [], [], []
    sends_across = core == odd

    for k in range(len(pieces)):
        if k >= 2:
            across[k - 2], pieces[k] = lax.optimization_barrier((across[k - 2], pieces[k]))
        across.append(permuted(pieces[k], partner_chip))
    swapped = permuted(blocks, partner_core)
    for k in range(len(pieces)):
        along.append(permuted(across[k], onward))
    for k in range(len(pieces)):
        handed = jnp.where(sends_across, across[k], along[k])
        passed.append(permuted(handed, partner_core))

    rows_of = {0: own_rows}
    for s in (1, -1, 2, -2):
        rows_of[s] = permuted(own_rows, lambda i, s=s: (i - s) % devices)

    def matches(s, g_rows):
        same = g_rows[:, :, None, None] == slab_cols[None, None, :, :]
        index = jnp.arange(same.shape[-1], dtype=jnp.int32)
        return jnp.max(jnp.where(same, index, -1), axis=-1).reshape(-1)

    out_shape = jax.ShapeDtypeStruct(
        (rows, freqs, parts, side, (2 * HALF + 1) * cols * side), jnp.bfloat16
    )
    q = jnp.arange(cols, dtype=jnp.int32)

    def step(sources, before):
        match = jnp.concatenate([matches(s, r) for s, r, _ in sources])
        place = jnp.concatenate([(s + HALF) * cols + q for s, _, _ in sources])
        chunks = [c for _, _, cs in sources for c in cs]
        return products(slab, match, place, chunks, out_shape, before)

    side_near = jnp.where(core == 0, 1, -1)
    rows_near = jnp.where(core == 0, rows_of[1], rows_of[-1])
    rows_far = jnp.where(core == 0, rows_of[-1], rows_of[1])
    side_across = jnp.where(odd == 0, 2, -2)
    rows_across = jnp.where(odd == 0, rows_of[2], rows_of[-2])
    rows_along = jnp.where(odd == 0, rows_of[-2], rows_of[2])

    out = step([(0, own_rows, [blocks]), (side_near, rows_near, [swapped])], None)
    out = step([(side_across, rows_across, across)], out)
    out = step([(-side_across, rows_along, along), (-side_near, rows_far, passed)], out)
    return out


def solution(mesh):
    placed = (
        P(("grp", "blk"), None, None, None, None, None),
        P("blk", None),
        P(("grp", "blk"), None, None, None, None, None),
        P("blk", None),
        P("blk"),
    )
    return jax.shard_map(
        shards,
        mesh=mesh,
        in_specs=placed,
        out_specs=P(("grp", "blk"), None, None, None, None),
        check_vma=False,
    )
```

```python
import functools

import jax
import jax.numpy as jnp
from jax import lax
from jax.experimental import pallas as pl
from jax.experimental.pallas import tpu as pltpu
from jax.sharding import PartitionSpec as P

HALF = 2
VMEM_BYTES = 16 * 2**20
CHUNKS = (2, 2, 2, 2)
CARRIER = 1
LIST_ROWS = 16
BASE = 128


def product_kernel(groups, arrays, slots, aliased, *refs):
    match_ref, place_ref, slab_ref = refs[:3]
    chunk_refs = refs[3 : 3 + arrays]
    refs = refs[3 + arrays + aliased :]
    out_ref, slab_v, block_v, total, out_v, slab_sem, block_sem, out_sem = refs
    rows, _, freqs = slab_ref.shape[:3]
    side = slab_ref.shape[4]
    sources = [
        ref.at[i, :, :, pl.ds(0, side)] for ref in chunk_refs for i in range(ref.shape[0])
    ]

    def needed(b):
        hit = match_ref[b * rows] >= 0
        for r in range(1, rows):
            hit = jnp.logical_or(hit, match_ref[b * rows + r] >= 0)
        return hit

    slab_copy = pltpu.make_async_copy(slab_ref, slab_v, slab_sem)
    slab_copy.start()
    for b, source in enumerate(sources):

        @pl.when(needed(b))
        def _():
            pltpu.make_async_copy(source, block_v.at[b], block_sem.at[b]).start()

    slab_copy.wait()

    def out_copy(g, r):
        return pltpu.make_async_copy(
            out_v.at[g, r],
            out_ref.at[r, :, :, :, pl.ds(pl.multiple_of(place_ref[g] * side, side), side)],
            out_sem.at[g, r],
        )

    def group(g, carry):
        total[...] = jnp.zeros_like(total)

        def slot(j, carry):
            b = g * slots + j

            @pl.when(needed(b))
            def _():
                pltpu.make_async_copy(block_v.at[b], block_v.at[b], block_sem.at[b]).wait()

            for r in range(rows):
                own = match_ref[b * rows + r]

                @pl.when(own >= 0)
                def _():
                    dot = functools.partial(jnp.dot, preferred_element_type=jnp.float32)
                    for f in range(freqs):
                        real, imag = slab_v[r, own, f, 0], slab_v[r, own, f, 1]
                        b_real, b_imag = block_v[b, f, 0], block_v[b, f, 1]
                        total[r, f, 0] += dot(real, b_real) - dot(imag, b_imag)
                        total[r, f, 1] += dot(real, b_imag) + dot(imag, b_real)

            return carry

        lax.fori_loop(0, slots, slot, 0)
        for r in range(rows):
            out_v[g, r] = total[r].astype(out_v.dtype)
            out_copy(g, r).start()
        return carry

    lax.fori_loop(0, groups, group, 0)

    def drain(g, carry):
        for r in range(rows):
            out_copy(g, r).wait()
        return carry

    lax.fori_loop(0, groups, drain, 0)


def products(slab, match, place, chunks, out_shape, before=None):
    rows, _, freqs, parts, side, _ = slab.shape
    groups = place.shape[0]
    slots = sum(chunk.shape[0] for chunk in chunks) // groups
    any_spec = pl.BlockSpec(memory_space=pl.ANY)
    smem_spec = pl.BlockSpec(memory_space=pltpu.SMEM)
    operands = [match, place, slab, *chunks] + ([] if before is None else [before])
    return pl.pallas_call(
        functools.partial(product_kernel, groups, len(chunks), slots, before is not None),
        out_shape=out_shape,
        in_specs=[smem_spec, smem_spec] + [any_spec] * (len(operands) - 2),
        out_specs=any_spec,
        scratch_shapes=[
            pltpu.VMEM(slab.shape, slab.dtype),
            pltpu.VMEM((groups * slots, freqs, parts, side, side), slab.dtype),
            pltpu.VMEM((rows, freqs, parts, side, side), jnp.float32),
            pltpu.VMEM((groups, rows, freqs, parts, side, side), out_shape.dtype),
            pltpu.SemaphoreType.DMA,
            pltpu.SemaphoreType.DMA((groups * slots,)),
            pltpu.SemaphoreType.DMA((groups, rows)),
        ],
        input_output_aliases={} if before is None else {len(operands) - 1: 0},
        compiler_params=pltpu.CompilerParams(vmem_limit_bytes=VMEM_BYTES),
        cost_estimate=pl.CostEstimate(
            flops=groups * slots * rows * 4 * freqs * side**3,
            bytes_accessed=2 * (slab.size + groups * (slots + rows) * freqs * parts * side * side),
            transcendentals=0,
        ),
    )(*operands)


def after(value, *others):
    return lax.optimization_barrier((value, *others))


def with_list(block, entries):
    flat = entries.reshape(-1) + BASE
    coded = jnp.stack([flat // BASE, flat % BASE]).astype(block.dtype)
    below = jnp.zeros(block.shape[:-2] + (LIST_ROWS, block.shape[-1]), block.dtype)
    below = lax.dynamic_update_slice(below, coded[None, None, None], (0,) * below.ndim)
    return jnp.concatenate([block, below], axis=-2)


def list_of(block, shape):
    count = shape[0] * shape[1]
    coded = block[0, 0, 0, -LIST_ROWS : -LIST_ROWS + 2, :count].astype(jnp.int32)
    return (coded[0] * BASE + coded[1] - BASE).reshape(shape)


def shards(slab, slab_cols, panels, panel_rows, panel_live):
    rows, _, freqs, parts, side, _ = slab.shape
    cols, slots = panel_rows.shape
    devices = lax.axis_size("blk")
    me = lax.axis_index("blk")
    core, odd = me % 2, (me // 2) % 2

    def permuted(value, target):
        return lax.ppermute(value, "blk", [(i, target(i)) for i in range(devices)])

    def partner_chip(i):
        return i ^ 2

    def partner_core(i):
        return i ^ 1

    def onward(i):
        return (i + 4 if (i // 2) % 2 == 0 else i - 4) % devices

    live = jnp.arange(slots, dtype=jnp.int32)[None, :] < panel_live[:, None]
    own_rows = jnp.where(live, panel_rows, -1)

    blocks = panels.reshape((cols * slots,) + panels.shape[2:])
    count = len(CHUNKS)
    edges = [sum(CHUNKS[:k]) for k in range(count + 1)]

    def cut(source, k):
        return source[edges[k] : edges[k + 1]]

    sends_across = core == odd

    def hand_over(first, last):
        handed = [
            jnp.where(sends_across, across[k][..., :side, :], along[k][..., :side, :])
            for k in range(first, last)
        ]
        return permuted(jnp.concatenate(handed), partner_core)

    def matches(s, g_rows):
        same = g_rows[:, :, None, None] == slab_cols[None, None, :, :]
        index = jnp.arange(same.shape[-1], dtype=jnp.int32)
        return jnp.max(jnp.where(same, index, -1), axis=-1).reshape(-1)

    out_shape = jax.ShapeDtypeStruct(
        (rows, freqs, parts, side, (2 * HALF + 1) * cols * side), jnp.bfloat16
    )
    q = jnp.arange(cols, dtype=jnp.int32)

    def step(sources, before):
        match = jnp.concatenate([matches(s, r) for s, r, _ in sources])
        place = jnp.concatenate([(s + HALF) * cols + q for s, _, _ in sources])
        chunks = [c for _, _, cs in sources for c in cs]
        return products(slab, match, place, chunks, out_shape, before)

    near = jnp.where(core == 0, 1, -1)
    over = jnp.where(odd == 0, 2, -2)

    piece = cut(blocks, 0)
    rest, piece = after(blocks, piece)
    pieces = [piece] + [cut(rest, k) for k in range(1, count)]
    pieces[CARRIER] = with_list(pieces[CARRIER], own_rows)
    across, along, passed = [], [], []
    for k in range(count):
        if k >= 2:
            across[k - 2], pieces[k] = after(across[k - 2], pieces[k])
        across.append(permuted(pieces[k], partner_chip))
    rows_across = list_of(across[CARRIER], own_rows.shape)
    whole, listed, across[1] = after(blocks, own_rows, across[1])
    swapped = permuted(whole, partner_core)
    rows_near = permuted(listed, partner_core)
    out = step([(0, own_rows, [blocks]), (near, rows_near, [swapped])], None)
    along.append(permuted(across[0], onward))
    along.append(permuted(across[1], onward))
    along.append(permuted(across[2], onward))
    along.append(permuted(across[3], onward))
    rows_along = list_of(along[CARRIER], own_rows.shape)
    rows_far = permuted(jnp.where(sends_across, rows_across, rows_along), partner_core)
    along[3], out = after(along[3], out)
    passed = [hand_over(0, 2), hand_over(2, 3), hand_over(3, 4)]
    out = step([(over, rows_across, across)], out)
    return step([(-over, rows_along, along), (-near, rows_far, passed)], out)

def solution(mesh):
    placed = (
        P(("grp", "blk"), None, None, None, None, None),
        P("blk", None),
        P(("grp", "blk"), None, None, None, None, None),
        P("blk", None),
        P("blk"),
    )
    return jax.shard_map(
        shards,
        mesh=mesh,
        in_specs=placed,
        out_specs=P(("grp", "blk"), None, None, None, None),
        check_vma=False,
    )
```

```python
import functools

import jax
import jax.numpy as jnp
from jax import lax
from jax.experimental import pallas as pl
from jax.experimental.pallas import tpu as pltpu
from jax.sharding import PartitionSpec as P

HALF = 2
CHUNK = 2
ONWARD = 3
EARLY = (3, 2)
VMEM_BYTES = 56 * 2**20


def gather_kernel(count, table_ref, own_ref, other_ref, *refs):
    *out_refs, held, sem, out_sem = refs
    chunk = out_refs[0].shape[0]

    def inward(source_ref, t):
        return pltpu.make_async_copy(source_ref.at[table_ref[2 * t + 1]], held.at[t], sem.at[t])

    def outward(t):
        target = out_refs[t // chunk].at[t % chunk]
        return pltpu.make_async_copy(held.at[t], target, out_sem.at[t])

    for t in range(count):

        @pl.when(table_ref[2 * t] == 0)
        def _():
            inward(own_ref, t).start()

        @pl.when(table_ref[2 * t] != 0)
        def _():
            inward(other_ref, t).start()

    for t in range(count):
        inward(own_ref, t).wait()
        outward(t).start()
    for t in range(count):
        outward(t).wait()


def gathered(table, own, other, chunks):
    shape = jax.ShapeDtypeStruct((CHUNK,) + own.shape[1:], own.dtype)
    any_spec = pl.BlockSpec(memory_space=pltpu.HBM)
    return pl.pallas_call(
        functools.partial(gather_kernel, chunks * CHUNK),
        out_shape=[shape] * chunks,
        in_specs=[pl.BlockSpec(memory_space=pltpu.SMEM), any_spec, any_spec],
        out_specs=[any_spec] * chunks,
        scratch_shapes=[
            pltpu.VMEM((chunks * CHUNK,) + own.shape[1:], own.dtype),
            pltpu.SemaphoreType.DMA((chunks * CHUNK,)),
            pltpu.SemaphoreType.DMA((chunks * CHUNK,)),
        ],
        compiler_params=pltpu.CompilerParams(vmem_limit_bytes=VMEM_BYTES),
    )(table, own, other)


def product_kernel(groups, slots, positions, total_positions, aliased, *refs):
    table_ref, slab_v = refs[:2]
    chunk_refs = refs[2 : 2 + len(positions)]
    refs = refs[2 + len(positions) + aliased :]
    out_ref, block_v, total, out_v, block_sem, out_sem = refs
    rows, _, freqs = slab_v.shape[:3]
    side = slab_v.shape[4]

    def match(b, r):
        return table_ref[total_positions + b * rows + r]

    def place(g):
        return table_ref[total_positions + groups * slots * rows + g]

    for start, ref in zip(positions, chunk_refs):
        for i in range(ref.shape[0]):
            target = table_ref[start + i]

            @pl.when(target >= 0)
            def _():
                pltpu.make_async_copy(
                    ref.at[i], block_v.at[target], block_sem.at[target]
                ).start()

    def out_copy(g, r):
        columns = pl.ds(pl.multiple_of(place(g) * side, side), side)
        return pltpu.make_async_copy(
            out_v.at[g, r], out_ref.at[r, :, :, :, columns], out_sem.at[g, r]
        )

    def product(b, r, own, p):
        for f in range(freqs):
            real, imag = block_v[b, f, 0], block_v[b, f, 1]
            both = jnp.concatenate([slab_v[r, own, f, 0], slab_v[r, own, f, 1]], axis=1)
            right = jnp.concatenate((imag, real) if p else (real, -imag))
            yield f, jnp.dot(both, right, preferred_element_type=jnp.float32)

    def row_panel(g, r):
        hits = [match(g * slots + j, r) for j in range(slots)]
        found = sum((hit >= 0).astype(jnp.int32) for hit in hits)

        @pl.when(found == 0)
        def _():
            out_v[g, r] = jnp.zeros(out_v.shape[2:], out_v.dtype)

        @pl.when(found == 1)
        def _():
            own = functools.reduce(jnp.maximum, hits)
            j = sum(jnp.where(hit >= 0, j, 0) for j, hit in enumerate(hits))
            for p in range(2):
                for f, value in product(g * slots + j, r, own, p):
                    out_v[g, r, f, p] = value.astype(out_v.dtype)

        @pl.when(found > 1)
        def _():
            total[...] = jnp.zeros_like(total)

            def add(j, carry):
                own = match(g * slots + j, r)

                @pl.when(own >= 0)
                def _():
                    for p in range(2):
                        for f, value in product(g * slots + j, r, own, p):
                            total[f, p] += value

                return carry

            lax.fori_loop(0, slots, add, 0)
            out_v[g, r] = total[...].astype(out_v.dtype)

        out_copy(g, r).start()

    def group(g, carry):
        @pl.when(place(g) >= 0)
        def _():
            for j in range(slots):
                b = g * slots + j

                @pl.when(functools.reduce(jnp.maximum, [match(b, r) for r in range(rows)]) >= 0)
                def _():
                    pltpu.make_async_copy(block_v.at[b], block_v.at[b], block_sem.at[b]).wait()

            for r in range(rows):
                row_panel(g, r)

        return carry

    def drain(g, carry):
        @pl.when(place(g) >= 0)
        def _():
            for r in range(rows):
                out_copy(g, r).wait()

        return carry

    lax.fori_loop(0, groups, group, 0)
    lax.fori_loop(0, groups, drain, 0)


def products(slab, table, groups, slots, total_positions, sources, out_shape, before=None):
    rows, _, freqs, parts, side, _ = slab.shape
    any_spec = pl.BlockSpec(memory_space=pltpu.HBM)
    operands = [table, slab, *(c for _, c in sources)] + ([] if before is None else [before])
    kernel = functools.partial(
        product_kernel, groups, slots, [p for p, _ in sources], total_positions, before is not None
    )
    return pl.pallas_call(
        kernel,
        out_shape=out_shape,
        in_specs=[pl.BlockSpec(memory_space=pltpu.SMEM), pl.BlockSpec(memory_space=pltpu.VMEM)]
        + [any_spec] * (len(operands) - 2),
        out_specs=any_spec,
        scratch_shapes=[
            pltpu.VMEM((groups * slots, freqs, parts, side, side), slab.dtype),
            pltpu.VMEM((freqs, parts, side, side), jnp.float32),
            pltpu.VMEM((groups, rows, freqs, parts, side, side), out_shape.dtype),
            pltpu.SemaphoreType.DMA((groups * slots,)),
            pltpu.SemaphoreType.DMA((groups, rows)),
        ],
        input_output_aliases={} if before is None else {len(operands) - 1: 0},
        compiler_params=pltpu.CompilerParams(vmem_limit_bytes=VMEM_BYTES),
    )(*operands)


def after(value, *others):
    return lax.optimization_barrier((value, *others))


def stations(rows, chip, cols, slots, devices):
    blocks = cols * slots
    index = jnp.arange(2 * blocks, dtype=jnp.int32)
    first = index % slots == 0
    reach = 2 * devices
    away = (rows - (4 * chip[..., None] + 2) + devices) % reach - devices
    away = jnp.where(chip[..., None] % 2 == 0, away, -away)
    key = jnp.where(rows >= 0, away, reach) * (2 * blocks) + index
    before = (key[..., None, :] < key[..., :, None]) & ~first
    rank = jnp.sum(before.astype(jnp.int32), axis=-1)
    own = index // blocks * blocks + index % blocks // slots
    dealt = rank % 2 * blocks + cols + rank // 2
    return jnp.where(first, own, dealt)


def shards(slab, slab_cols, panels, panel_rows, panel_live):
    rows, _, freqs, parts, side, _ = slab.shape
    cols, slots = panel_rows.shape
    count = cols * slots
    chunks = count // CHUNK
    devices = lax.axis_size("blk")
    chips = devices // 2
    me = lax.axis_index("blk")
    core, chip = me % 2, me // 2
    toward = jnp.where(chip % 2 == 0, 1, -1)

    def permuted(value, target):
        return lax.ppermute(value, "blk", [(i, target(i)) for i in range(devices)])

    def partner_chip(i):
        return i ^ 2

    def partner_core(i):
        return i ^ 1

    def onward(i):
        return (i + 4 if (i // 2) % 2 == 0 else i - 4) % devices

    live = jnp.arange(slots, dtype=jnp.int32)[None, :] < panel_live[:, None]
    own_rows = jnp.where(live, panel_rows, -1).reshape(-1)
    own_lists = jnp.concatenate([own_rows, slab_cols.reshape(-1)])[None]

    def doubled(lists):
        size = lists.shape[0]
        others = permuted(lists, lambda i: i ^ size)
        low = (me // size) % 2 == 0
        return jnp.where(
            low, jnp.concatenate([lists, others]), jnp.concatenate([others, lists])
        )

    blocks = panels.reshape((count,) + panels.shape[2:])
    across = [permuted(panels[:, 0], partner_chip)]
    lists = doubled(own_lists)
    other = permuted(blocks, partner_core)

    pair = lists[:, :count].reshape(-1)
    other_rows = jnp.where(core == 0, lists[1, :count], lists[0, :count])
    station = stations(pair, chip, cols, slots, devices)
    wanted = core * count + jnp.arange(CHUNK, count, dtype=jnp.int32)
    index = jnp.arange(2 * count, dtype=jnp.int32)
    picked = jnp.sum(jnp.where(station[None] == wanted[:, None], index, 0), axis=1)
    table = jnp.stack([jnp.abs(picked // count - core), picked % count], axis=1).reshape(-1)
    pieces = list(gathered(table, blocks, other, chunks - 1))

    across.append(permuted(pieces[0], partner_chip))
    for k in range(2, chunks):
        if k == 2:
            lists = doubled(lists)
            lists, pieces[k - 1] = after(lists, pieces[k - 1])
        across[k - 2], pieces[k - 1] = after(across[k - 2], pieces[k - 1])
        across.append(permuted(pieces[k - 1], partner_chip))
    along = [permuted(across[k], onward) for k in range(ONWARD - 1)]
    while lists.shape[0] < devices:
        lists = doubled(lists)
    across[ONWARD - 1], lists = after(across[ONWARD - 1], lists)
    along.append(permuted(across[ONWARD - 1], onward))

    all_rows = lists[:, :count].reshape(chips, 2 * count)
    all_cols = lists[:, count:].reshape(chips, 2, -1)
    all_chips = jnp.arange(chips, dtype=jnp.int32)
    all_stations = stations(all_rows, all_chips, cols, slots, devices)

    def meets(found):
        same = found[..., None, None] == slab_cols
        order = jnp.arange(slab_cols.shape[1], dtype=jnp.int32)
        return jnp.max(jnp.where(same, order, -1), axis=-1)

    out_shape = jax.ShapeDtypeStruct(
        (rows, freqs, parts, side, (2 * HALF + 1) * cols * side), jnp.bfloat16
    )
    q = jnp.arange(cols, dtype=jnp.int32)

    def table_of(position, match, place, total_positions):
        match = jnp.where((place >= 0)[:, None, None], match, -1)
        used = jnp.any(match >= 0, axis=-1).reshape(-1)
        at = jnp.arange(total_positions, dtype=jnp.int32)
        here = (position.reshape(-1)[None, :] == at[:, None]) & used
        target = jnp.max(jnp.where(here, jnp.arange(used.size, dtype=jnp.int32), -1), axis=1)
        return jnp.concatenate([target, match.reshape(-1), place]).astype(jnp.int32)

    near = jnp.stack([jnp.zeros_like(me), 1 - 2 * core])
    place = ((near + HALF)[:, None] * cols + q).reshape(-1)
    position = jnp.arange(2 * count, dtype=jnp.int32).reshape(2 * cols, slots)
    match = meets(jnp.concatenate([own_rows, other_rows]).reshape(2 * cols, slots))
    out = products(
        slab,
        table_of(position, match, place, 2 * count),
        2 * cols,
        slots,
        2 * count,
        [(0, blocks), (count, other)],
        out_shape,
    )

    sources = jnp.stack([chip + toward, (chip - toward) % chips])
    offset = jnp.stack([2 * toward, -2 * toward])[:, None] + jnp.arange(2) - core
    found = all_rows[sources].reshape(4 * cols, slots)
    station = all_stations[sources]
    position = station % count + jnp.where(station // count == core, 0, count)
    position += 2 * count * jnp.arange(2, dtype=jnp.int32)[:, None]
    position = position.reshape(4 * cols, slots)
    match = meets(found)
    match = jnp.where((found >= 0)[..., None], match, -1)
    place = jnp.where(jnp.abs(offset) <= HALF, offset + HALF, -1)
    place = jnp.where(place[..., None] >= 0, place[..., None] * cols + q, -1).reshape(-1)
    used = jnp.any(match >= 0, axis=-1)
    turn = position % count // CHUNK
    from_z = position >= 2 * count

    def ready(limits):
        return jnp.all(~used | (turn < jnp.where(from_z, limits[1], limits[0])), axis=1)

    early, usual = ready(EARLY), ready((chunks, ONWARD))
    total_positions = 4 * count

    def step(chosen, parts_held, before):
        sources = [
            (kind * count + k * CHUNK, c) for kind, held in enumerate(parts_held) for k, c in enumerate(held)
        ]
        table = table_of(position, match, jnp.where(chosen, place, -1), total_positions)
        return products(
            slab, table, 4 * cols, slots, total_positions, sources, out_shape, before
        )

    across_other = [permuted(c, partner_core) for c in across]
    along_other = [permuted(c, partner_core) for c in along]
    a, b = EARLY
    held = (across, across_other, along, along_other)
    out = step(usual, held, out)

    late = all_stations % count // CHUNK >= ONWARD
    back = jnp.where(all_chips % 2 == 0, -1, 1)
    readers = all_cols[(all_chips + back) % chips]
    hit = jnp.any(all_rows[:, :, None, None] == readers[:, None], axis=-1)
    of_core = index[:, None] // count - jnp.arange(2)
    within = jnp.abs(of_core - 2 * back[:, None, None]) <= HALF
    rare = jnp.any(hit & within & (late & (all_rows >= 0))[..., None])

    def complete(out):
        more = [permuted(c, onward) for c in across[ONWARD:]]
        more_other = [permuted(c, partner_core) for c in more]
        return step(~usual, (across, across_other, along + more, along_other + more_other), out)

    return lax.cond(rare, complete, lambda out: out, out)


def solution(mesh):
    placed = (
        P(("grp", "blk"), None, None, None, None, None),
        P("blk", None),
        P(("grp", "blk"), None, None, None, None, None),
        P("blk", None),
        P("blk"),
    )
    return jax.shard_map(
        shards,
        mesh=mesh,
        in_specs=placed,
        out_specs=P(("grp", "blk"), None, None, None, None),
        check_vma=False,
    )
```

```python
import functools

import jax
import jax.numpy as jnp
from jax import lax
from jax.experimental import pallas as pl
from jax.experimental.pallas import tpu as pltpu
from jax.sharding import PartitionSpec as P

HALF = 2
CHUNK = 2
ONWARD = 3
EARLY = (3, 2)
VMEM_BYTES = 56 * 2**20


def gather_kernel(count, table_ref, own_ref, other_ref, *refs):
    *out_refs, held, sem, out_sem = refs
    chunk = out_refs[0].shape[0]

    def inward(source_ref, t):
        return pltpu.make_async_copy(source_ref.at[table_ref[2 * t + 1]], held.at[t], sem.at[t])

    def outward(t):
        target = out_refs[t // chunk].at[t % chunk]
        return pltpu.make_async_copy(held.at[t], target, out_sem.at[t])

    for t in range(count):

        @pl.when(table_ref[2 * t] == 0)
        def _():
            inward(own_ref, t).start()

        @pl.when(table_ref[2 * t] != 0)
        def _():
            inward(other_ref, t).start()

    for t in range(count):
        inward(own_ref, t).wait()
        outward(t).start()
    for t in range(count):
        outward(t).wait()


def gathered(table, own, other, chunks):
    shape = jax.ShapeDtypeStruct((CHUNK,) + own.shape[1:], own.dtype)
    any_spec = pl.BlockSpec(memory_space=pltpu.HBM)
    return pl.pallas_call(
        functools.partial(gather_kernel, chunks * CHUNK),
        out_shape=[shape] * chunks,
        in_specs=[pl.BlockSpec(memory_space=pltpu.SMEM), any_spec, any_spec],
        out_specs=[any_spec] * chunks,
        scratch_shapes=[
            pltpu.VMEM((chunks * CHUNK,) + own.shape[1:], own.dtype),
            pltpu.SemaphoreType.DMA((chunks * CHUNK,)),
            pltpu.SemaphoreType.DMA((chunks * CHUNK,)),
        ],
        compiler_params=pltpu.CompilerParams(vmem_limit_bytes=VMEM_BYTES),
    )(table, own, other)


def product_kernel(groups, slots, positions, total_positions, aliased, *refs):
    table_ref, slab_v = refs[:2]
    chunk_refs = refs[2 : 2 + len(positions)]
    refs = refs[2 + len(positions) + aliased :]
    out_ref, block_v, total, out_v, block_sem, out_sem = refs
    rows, _, freqs = slab_v.shape[:3]
    side = slab_v.shape[4]

    def match(b, r):
        return table_ref[total_positions + b * rows + r]

    def place(g):
        return table_ref[total_positions + groups * slots * rows + g]

    for start, ref in zip(positions, chunk_refs):
        for i in range(ref.shape[0]):
            target = table_ref[start + i]

            @pl.when(target >= 0)
            def _():
                pltpu.make_async_copy(
                    ref.at[i], block_v.at[target], block_sem.at[target]
                ).start()

    def out_copy(g, r):
        columns = pl.ds(pl.multiple_of(place(g) * side, side), side)
        return pltpu.make_async_copy(
            out_v.at[g, r], out_ref.at[r, :, :, :, columns], out_sem.at[g, r]
        )

    def product(b, r, own, p):
        for f in range(freqs):
            real, imag = block_v[b, f, 0], block_v[b, f, 1]
            both = jnp.concatenate([slab_v[r, own, f, 0], slab_v[r, own, f, 1]], axis=1)
            right = jnp.concatenate((imag, real) if p else (real, -imag))
            yield f, jnp.dot(both, right, preferred_element_type=jnp.float32)

    def row_panel(g, r):
        hits = [match(g * slots + j, r) for j in range(slots)]
        found = sum((hit >= 0).astype(jnp.int32) for hit in hits)

        @pl.when(found == 0)
        def _():
            out_v[g, r] = jnp.zeros(out_v.shape[2:], out_v.dtype)

        @pl.when(found == 1)
        def _():
            own = functools.reduce(jnp.maximum, hits)
            j = sum(jnp.where(hit >= 0, j, 0) for j, hit in enumerate(hits))
            for p in range(2):
                for f, value in product(g * slots + j, r, own, p):
                    out_v[g, r, f, p] = value.astype(out_v.dtype)

        @pl.when(found > 1)
        def _():
            total[...] = jnp.zeros_like(total)

            def add(j, carry):
                own = match(g * slots + j, r)

                @pl.when(own >= 0)
                def _():
                    for p in range(2):
                        for f, value in product(g * slots + j, r, own, p):
                            total[f, p] += value

                return carry

            lax.fori_loop(0, slots, add, 0)
            out_v[g, r] = total[...].astype(out_v.dtype)

        out_copy(g, r).start()

    def group(g, carry):
        @pl.when(place(g) >= 0)
        def _():
            for j in range(slots):
                b = g * slots + j

                @pl.when(functools.reduce(jnp.maximum, [match(b, r) for r in range(rows)]) >= 0)
                def _():
                    pltpu.make_async_copy(block_v.at[b], block_v.at[b], block_sem.at[b]).wait()

            for r in range(rows):
                row_panel(g, r)

        return carry

    def drain(g, carry):
        @pl.when(place(g) >= 0)
        def _():
            for r in range(rows):
                out_copy(g, r).wait()

        return carry

    lax.fori_loop(0, groups, group, 0)
    lax.fori_loop(0, groups, drain, 0)


def products(slab, table, groups, slots, total_positions, sources, out_shape, before=None):
    rows, _, freqs, parts, side, _ = slab.shape
    any_spec = pl.BlockSpec(memory_space=pltpu.HBM)
    operands = [table, slab, *(c for _, c in sources)] + ([] if before is None else [before])
    kernel = functools.partial(
        product_kernel, groups, slots, [p for p, _ in sources], total_positions, before is not None
    )
    return pl.pallas_call(
        kernel,
        out_shape=out_shape,
        in_specs=[pl.BlockSpec(memory_space=pltpu.SMEM), pl.BlockSpec(memory_space=pltpu.VMEM)]
        + [any_spec] * (len(operands) - 2),
        out_specs=any_spec,
        scratch_shapes=[
            pltpu.VMEM((groups * slots, freqs, parts, side, side), slab.dtype),
            pltpu.VMEM((freqs, parts, side, side), jnp.float32),
            pltpu.VMEM((groups, rows, freqs, parts, side, side), out_shape.dtype),
            pltpu.SemaphoreType.DMA((groups * slots,)),
            pltpu.SemaphoreType.DMA((groups, rows)),
        ],
        input_output_aliases={} if before is None else {len(operands) - 1: 0},
        compiler_params=pltpu.CompilerParams(vmem_limit_bytes=VMEM_BYTES),
    )(*operands)


def after(value, *others):
    return lax.optimization_barrier((value, *others))


def stations(rows, chip, cols, slots, devices):
    blocks = cols * slots
    index = jnp.arange(2 * blocks, dtype=jnp.int32)
    first = index % slots == 0
    reach = 2 * devices
    away = (rows - (4 * chip[..., None] + 2) + devices) % reach - devices
    away = jnp.where(chip[..., None] % 2 == 0, away, -away)
    key = jnp.where(rows >= 0, away, reach) * (2 * blocks) + index
    before = (key[..., None, :] < key[..., :, None]) & ~first
    rank = jnp.sum(before.astype(jnp.int32), axis=-1)
    own = index // blocks * blocks + index % blocks // slots
    dealt = rank % 2 * blocks + cols + rank // 2
    return jnp.where(first, own, dealt)


def shards(slab, slab_cols, panels, panel_rows, panel_live):
    rows, _, freqs, parts, side, _ = slab.shape
    cols, slots = panel_rows.shape
    count = cols * slots
    chunks = count // CHUNK
    devices = lax.axis_size("blk")
    chips = devices // 2
    me = lax.axis_index("blk")
    core, chip = me % 2, me // 2
    toward = jnp.where(chip % 2 == 0, 1, -1)

    def permuted(value, target):
        return lax.ppermute(value, "blk", [(i, target(i)) for i in range(devices)])

    def partner_chip(i):
        return i ^ 2

    def partner_core(i):
        return i ^ 1

    def onward(i):
        return (i + 4 if (i // 2) % 2 == 0 else i - 4) % devices

    live = jnp.arange(slots, dtype=jnp.int32)[None, :] < panel_live[:, None]
    own_rows = jnp.where(live, panel_rows, -1).reshape(-1)
    own_lists = jnp.concatenate([own_rows, slab_cols.reshape(-1)])[None]

    def doubled(lists):
        size = lists.shape[0]
        others = permuted(lists, lambda i: i ^ size)
        low = (me // size) % 2 == 0
        return jnp.where(
            low, jnp.concatenate([lists, others]), jnp.concatenate([others, lists])
        )

    blocks = panels.reshape((count,) + panels.shape[2:])
    piece, own_lists = after(panels[:, 0], own_lists)
    across = [permuted(piece, partner_chip)]
    lists = doubled(own_lists)
    other = permuted(blocks, partner_core)

    pair = lists[:, :count].reshape(-1)
    other_rows = jnp.where(core == 0, lists[1, :count], lists[0, :count])
    station = stations(pair, chip, cols, slots, devices)
    wanted = core * count + jnp.arange(CHUNK, count, dtype=jnp.int32)
    index = jnp.arange(2 * count, dtype=jnp.int32)
    picked = jnp.sum(jnp.where(station[None] == wanted[:, None], index, 0), axis=1)
    table = jnp.stack([jnp.abs(picked // count - core), picked % count], axis=1).reshape(-1)
    pieces = list(gathered(table, blocks, other, chunks - 1))

    across.append(permuted(pieces[0], partner_chip))
    for k in range(2, chunks):
        if k == 3:
            lists = doubled(lists)
            lists, pieces[k - 1] = after(lists, pieces[k - 1])
        across[k - 2], pieces[k - 1] = after(across[k - 2], pieces[k - 1])
        across.append(permuted(pieces[k - 1], partner_chip))
    along = [permuted(across[k], onward) for k in range(ONWARD - 1)]
    while lists.shape[0] < devices:
        lists = doubled(lists)
    across[ONWARD - 1], lists = after(across[ONWARD - 1], lists)
    along.append(permuted(across[ONWARD - 1], onward))

    all_rows = lists[:, :count].reshape(chips, 2 * count)
    all_cols = lists[:, count:].reshape(chips, 2, -1)
    all_chips = jnp.arange(chips, dtype=jnp.int32)
    all_stations = stations(all_rows, all_chips, cols, slots, devices)

    def meets(found):
        same = found[..., None, None] == slab_cols
        order = jnp.arange(slab_cols.shape[1], dtype=jnp.int32)
        return jnp.max(jnp.where(same, order, -1), axis=-1)

    out_shape = jax.ShapeDtypeStruct(
        (rows, freqs, parts, side, (2 * HALF + 1) * cols * side), jnp.bfloat16
    )
    q = jnp.arange(cols, dtype=jnp.int32)

    def table_of(position, match, place, total_positions):
        match = jnp.where((place >= 0)[:, None, None], match, -1)
        used = jnp.any(match >= 0, axis=-1).reshape(-1)
        at = jnp.arange(total_positions, dtype=jnp.int32)
        here = (position.reshape(-1)[None, :] == at[:, None]) & used
        target = jnp.max(jnp.where(here, jnp.arange(used.size, dtype=jnp.int32), -1), axis=1)
        return jnp.concatenate([target, match.reshape(-1), place]).astype(jnp.int32)

    near = jnp.stack([jnp.zeros_like(me), 1 - 2 * core])
    place = ((near + HALF)[:, None] * cols + q).reshape(-1)
    position = jnp.arange(2 * count, dtype=jnp.int32).reshape(2 * cols, slots)
    match = meets(jnp.concatenate([own_rows, other_rows]).reshape(2 * cols, slots))
    out = products(
        slab,
        table_of(position, match, place, 2 * count),
        2 * cols,
        slots,
        2 * count,
        [(0, blocks), (count, other)],
        out_shape,
    )

    sources = jnp.stack([chip + toward, (chip - toward) % chips])
    offset = jnp.stack([2 * toward, -2 * toward])[:, None] + jnp.arange(2) - core
    found = all_rows[sources].reshape(4 * cols, slots)
    station = all_stations[sources]
    position = station % count + jnp.where(station // count == core, 0, count)
    position += 2 * count * jnp.arange(2, dtype=jnp.int32)[:, None]
    position = position.reshape(4 * cols, slots)
    match = meets(found)
    match = jnp.where((found >= 0)[..., None], match, -1)
    place = jnp.where(jnp.abs(offset) <= HALF, offset + HALF, -1)
    place = jnp.where(place[..., None] >= 0, place[..., None] * cols + q, -1).reshape(-1)
    used = jnp.any(match >= 0, axis=-1)
    turn = position % count // CHUNK
    from_z = position >= 2 * count

    def ready(limits):
        return jnp.all(~used | (turn < jnp.where(from_z, limits[1], limits[0])), axis=1)

    early, usual = ready(EARLY), ready((chunks, ONWARD))
    total_positions = 4 * count

    def step(chosen, parts_held, before):
        sources = [
            (kind * count + k * CHUNK, c) for kind, held in enumerate(parts_held) for k, c in enumerate(held)
        ]
        table = table_of(position, match, jnp.where(chosen, place, -1), total_positions)
        return products(
            slab, table, 4 * cols, slots, total_positions, sources, out_shape, before
        )

    across_other = [permuted(c, partner_core) for c in across]
    along_other = [permuted(c, partner_core) for c in along]
    a, b = EARLY
    held = (across, across_other, along, along_other)
    out = step(usual, held, out)

    late = all_stations % count // CHUNK >= ONWARD
    back = jnp.where(all_chips % 2 == 0, -1, 1)
    readers = all_cols[(all_chips + back) % chips]
    hit = jnp.any(all_rows[:, :, None, None] == readers[:, None], axis=-1)
    of_core = index[:, None] // count - jnp.arange(2)
    within = jnp.abs(of_core - 2 * back[:, None, None]) <= HALF
    rare = jnp.any(hit & within & (late & (all_rows >= 0))[..., None])

    def complete(out):
        more = [permuted(c, onward) for c in across[ONWARD:]]
        more_other = [permuted(c, partner_core) for c in more]
        return step(~usual, (across, across_other, along + more, along_other + more_other), out)

    return lax.cond(rare, complete, lambda out: out, out)


def solution(mesh):
    placed = (
        P(("grp", "blk"), None, None, None, None, None),
        P("blk", None),
        P(("grp", "blk"), None, None, None, None, None),
        P("blk", None),
        P("blk"),
    )
    return jax.shard_map(
        shards,
        mesh=mesh,
        in_specs=placed,
        out_specs=P(("grp", "blk"), None, None, None, None),
        check_vma=False,
    )
```

```python
import functools

import jax
import jax.numpy as jnp
from jax import lax
from jax.experimental import pallas as pl
from jax.experimental.pallas import tpu as pltpu
from jax.sharding import PartitionSpec as P

HALF = 2
CHUNK = 2
ONWARD = 3
EARLY = (3, 2)
VMEM_BYTES = 56 * 2**20


def gather_kernel(count, table_ref, own_ref, other_ref, *refs):
    *out_refs, held, sem, out_sem = refs
    chunk = out_refs[0].shape[0]

    def inward(source_ref, t):
        return pltpu.make_async_copy(source_ref.at[table_ref[2 * t + 1]], held.at[t], sem.at[t])

    def outward(t):
        target = out_refs[t // chunk].at[t % chunk]
        return pltpu.make_async_copy(held.at[t], target, out_sem.at[t])

    for t in range(count):

        @pl.when(table_ref[2 * t] == 0)
        def _():
            inward(own_ref, t).start()

        @pl.when(table_ref[2 * t] != 0)
        def _():
            inward(other_ref, t).start()

    for t in range(count):
        inward(own_ref, t).wait()
        outward(t).start()
    for t in range(count):
        outward(t).wait()


def gathered(table, own, other, chunks):
    shape = jax.ShapeDtypeStruct((CHUNK,) + own.shape[1:], own.dtype)
    any_spec = pl.BlockSpec(memory_space=pltpu.HBM)
    return pl.pallas_call(
        functools.partial(gather_kernel, chunks * CHUNK),
        out_shape=[shape] * chunks,
        in_specs=[pl.BlockSpec(memory_space=pltpu.SMEM), any_spec, any_spec],
        out_specs=[any_spec] * chunks,
        scratch_shapes=[
            pltpu.VMEM((chunks * CHUNK,) + own.shape[1:], own.dtype),
            pltpu.SemaphoreType.DMA((chunks * CHUNK,)),
            pltpu.SemaphoreType.DMA((chunks * CHUNK,)),
        ],
        compiler_params=pltpu.CompilerParams(vmem_limit_bytes=VMEM_BYTES),
    )(table, own, other)


def product_kernel(groups, slots, positions, total_positions, aliased, *refs):
    table_ref, slab_v = refs[:2]
    chunk_refs = refs[2 : 2 + len(positions)]
    refs = refs[2 + len(positions) + aliased :]
    out_ref, block_v, total, out_v, block_sem, out_sem = refs
    rows, _, freqs = slab_v.shape[:3]
    side = slab_v.shape[4]

    def match(b, r):
        return table_ref[total_positions + b * rows + r]

    def place(g):
        return table_ref[total_positions + groups * slots * rows + g]

    for start, ref in zip(positions, chunk_refs):
        for i in range(ref.shape[0]):
            target = table_ref[start + i]

            @pl.when(target >= 0)
            def _():
                pltpu.make_async_copy(
                    ref.at[i], block_v.at[target], block_sem.at[target]
                ).start()

    def out_copy(g, r):
        columns = pl.ds(pl.multiple_of(place(g) * side, side), side)
        return pltpu.make_async_copy(
            out_v.at[g, r], out_ref.at[r, :, :, :, columns], out_sem.at[g, r]
        )

    def product(b, r, own, p):
        for f in range(freqs):
            real, imag = block_v[b, f, 0], block_v[b, f, 1]
            both = jnp.concatenate([slab_v[r, own, f, 0], slab_v[r, own, f, 1]], axis=1)
            right = jnp.concatenate((imag, real) if p else (real, -imag))
            yield f, jnp.dot(both, right, preferred_element_type=jnp.float32)

    def row_panel(g, r):
        hits = [match(g * slots + j, r) for j in range(slots)]
        found = sum((hit >= 0).astype(jnp.int32) for hit in hits)

        @pl.when(found == 0)
        def _():
            out_v[g, r] = jnp.zeros(out_v.shape[2:], out_v.dtype)

        @pl.when(found == 1)
        def _():
            own = functools.reduce(jnp.maximum, hits)
            j = sum(jnp.where(hit >= 0, j, 0) for j, hit in enumerate(hits))
            for p in range(2):
                for f, value in product(g * slots + j, r, own, p):
                    out_v[g, r, f, p] = value.astype(out_v.dtype)

        @pl.when(found == 2)
        def _():
            first = last = jnp.int32(0)
            for j, hit in enumerate(hits):
                last = jnp.where(hit >= 0, j, last)
            for j in reversed(range(slots)):
                first = jnp.where(hits[j] >= 0, j, first)
            picks = [(g * slots + j, match(g * slots + j, r)) for j in (first, last)]
            for f in range(freqs):
                left = jnp.concatenate(
                    [slab_v[r, own, f, p] for _, own in picks for p in range(2)], axis=1
                )
                for p in range(2):
                    right = []
                    for b, _ in picks:
                        real, imag = block_v[b, f, 0], block_v[b, f, 1]
                        right += [imag, real] if p else [real, -imag]
                    value = jnp.dot(
                        left, jnp.concatenate(right), preferred_element_type=jnp.float32
                    )
                    out_v[g, r, f, p] = value.astype(out_v.dtype)

        @pl.when(found > 2)
        def _():
            total[...] = jnp.zeros_like(total)

            def add(j, carry):
                own = match(g * slots + j, r)

                @pl.when(own >= 0)
                def _():
                    for p in range(2):
                        for f, value in product(g * slots + j, r, own, p):
                            total[f, p] += value

                return carry

            lax.fori_loop(0, slots, add, 0)
            out_v[g, r] = total[...].astype(out_v.dtype)

        out_copy(g, r).start()

    def group(g, carry):
        @pl.when(place(g) >= 0)
        def _():
            for j in range(slots):
                b = g * slots + j

                @pl.when(functools.reduce(jnp.maximum, [match(b, r) for r in range(rows)]) >= 0)
                def _():
                    pltpu.make_async_copy(block_v.at[b], block_v.at[b], block_sem.at[b]).wait()

            for r in range(rows):
                row_panel(g, r)

        return carry

    def drain(g, carry):
        @pl.when(place(g) >= 0)
        def _():
            for r in range(rows):
                out_copy(g, r).wait()

        return carry

    lax.fori_loop(0, groups, group, 0)
    lax.fori_loop(0, groups, drain, 0)


def products(slab, table, groups, slots, total_positions, sources, out_shape, before=None):
    rows, _, freqs, parts, side, _ = slab.shape
    any_spec = pl.BlockSpec(memory_space=pltpu.HBM)
    operands = [table, slab, *(c for _, c in sources)] + ([] if before is None else [before])
    kernel = functools.partial(
        product_kernel, groups, slots, [p for p, _ in sources], total_positions, before is not None
    )
    return pl.pallas_call(
        kernel,
        out_shape=out_shape,
        in_specs=[pl.BlockSpec(memory_space=pltpu.SMEM), pl.BlockSpec(memory_space=pltpu.VMEM)]
        + [any_spec] * (len(operands) - 2),
        out_specs=any_spec,
        scratch_shapes=[
            pltpu.VMEM((groups * slots, freqs, parts, side, side), slab.dtype),
            pltpu.VMEM((freqs, parts, side, side), jnp.float32),
            pltpu.VMEM((groups, rows, freqs, parts, side, side), out_shape.dtype),
            pltpu.SemaphoreType.DMA((groups * slots,)),
            pltpu.SemaphoreType.DMA((groups, rows)),
        ],
        input_output_aliases={} if before is None else {len(operands) - 1: 0},
        compiler_params=pltpu.CompilerParams(vmem_limit_bytes=VMEM_BYTES),
    )(*operands)


def after(value, *others):
    return lax.optimization_barrier((value, *others))


def stations(rows, chip, cols, slots, devices):
    blocks = cols * slots
    index = jnp.arange(2 * blocks, dtype=jnp.int32)
    first = index % slots == 0
    reach = 2 * devices
    away = (rows - (4 * chip[..., None] + 2) + devices) % reach - devices
    away = jnp.where(chip[..., None] % 2 == 0, away, -away)
    key = jnp.where(rows >= 0, away, reach) * (2 * blocks) + index
    before = (key[..., None, :] < key[..., :, None]) & ~first
    rank = jnp.sum(before.astype(jnp.int32), axis=-1)
    own = index // blocks * blocks + index % blocks // slots
    dealt = rank % 2 * blocks + cols + rank // 2
    return jnp.where(first, own, dealt)


def shards(slab, slab_cols, panels, panel_rows, panel_live):
    rows, _, freqs, parts, side, _ = slab.shape
    cols, slots = panel_rows.shape
    count = cols * slots
    chunks = count // CHUNK
    devices = lax.axis_size("blk")
    chips = devices // 2
    me = lax.axis_index("blk")
    core, chip = me % 2, me // 2
    toward = jnp.where(chip % 2 == 0, 1, -1)

    def permuted(value, target):
        return lax.ppermute(value, "blk", [(i, target(i)) for i in range(devices)])

    def partner_chip(i):
        return i ^ 2

    def partner_core(i):
        return i ^ 1

    def onward(i):
        return (i + 4 if (i // 2) % 2 == 0 else i - 4) % devices

    live = jnp.arange(slots, dtype=jnp.int32)[None, :] < panel_live[:, None]
    own_rows = jnp.where(live, panel_rows, -1).reshape(-1)
    own_lists = jnp.concatenate([own_rows, slab_cols.reshape(-1)])[None]

    def doubled(lists):
        size = lists.shape[0]
        others = permuted(lists, lambda i: i ^ size)
        low = (me // size) % 2 == 0
        return jnp.where(
            low, jnp.concatenate([lists, others]), jnp.concatenate([others, lists])
        )

    blocks = panels.reshape((count,) + panels.shape[2:])
    piece, own_lists = after(panels[:, 0], own_lists)
    across = [permuted(piece, partner_chip)]
    lists = doubled(own_lists)
    other = permuted(blocks, partner_core)

    pair = lists[:, :count].reshape(-1)
    other_rows = jnp.where(core == 0, lists[1, :count], lists[0, :count])
    station = stations(pair, chip, cols, slots, devices)
    wanted = core * count + jnp.arange(CHUNK, count, dtype=jnp.int32)
    index = jnp.arange(2 * count, dtype=jnp.int32)
    picked = jnp.sum(jnp.where(station[None] == wanted[:, None], index, 0), axis=1)
    table = jnp.stack([jnp.abs(picked // count - core), picked % count], axis=1).reshape(-1)
    pieces = list(gathered(table, blocks, other, chunks - 1))

    across.append(permuted(pieces[0], partner_chip))
    for k in range(2, chunks):
        if k == 3:
            lists = doubled(lists)
            lists, pieces[k - 1] = after(lists, pieces[k - 1])
        across[k - 2], pieces[k - 1] = after(across[k - 2], pieces[k - 1])
        across.append(permuted(pieces[k - 1], partner_chip))
    along = [permuted(across[k], onward) for k in range(ONWARD - 1)]
    while lists.shape[0] < devices:
        lists = doubled(lists)
    across[ONWARD - 1], lists = after(across[ONWARD - 1], lists)
    along.append(permuted(across[ONWARD - 1], onward))

    all_rows = lists[:, :count].reshape(chips, 2 * count)
    all_cols = lists[:, count:].reshape(chips, 2, -1)
    all_chips = jnp.arange(chips, dtype=jnp.int32)
    all_stations = stations(all_rows, all_chips, cols, slots, devices)

    def meets(found):
        same = found[..., None, None] == slab_cols
        order = jnp.arange(slab_cols.shape[1], dtype=jnp.int32)
        return jnp.max(jnp.where(same, order, -1), axis=-1)

    out_shape = jax.ShapeDtypeStruct(
        (rows, freqs, parts, side, (2 * HALF + 1) * cols * side), jnp.bfloat16
    )
    q = jnp.arange(cols, dtype=jnp.int32)

    def table_of(position, match, place, total_positions):
        match = jnp.where((place >= 0)[:, None, None], match, -1)
        used = jnp.any(match >= 0, axis=-1).reshape(-1)
        at = jnp.arange(total_positions, dtype=jnp.int32)
        here = (position.reshape(-1)[None, :] == at[:, None]) & used
        target = jnp.max(jnp.where(here, jnp.arange(used.size, dtype=jnp.int32), -1), axis=1)
        return jnp.concatenate([target, match.reshape(-1), place]).astype(jnp.int32)

    near = jnp.stack([jnp.zeros_like(me), 1 - 2 * core])
    place = ((near + HALF)[:, None] * cols + q).reshape(-1)
    position = jnp.arange(2 * count, dtype=jnp.int32).reshape(2 * cols, slots)
    match = meets(jnp.concatenate([own_rows, other_rows]).reshape(2 * cols, slots))
    out = products(
        slab,
        table_of(position, match, place, 2 * count),
        2 * cols,
        slots,
        2 * count,
        [(0, blocks), (count, other)],
        out_shape,
    )

    sources = jnp.stack([chip + toward, (chip - toward) % chips])
    offset = jnp.stack([2 * toward, -2 * toward])[:, None] + jnp.arange(2) - core
    found = all_rows[sources].reshape(4 * cols, slots)
    station = all_stations[sources]
    position = station % count + jnp.where(station // count == core, 0, count)
    position += 2 * count * jnp.arange(2, dtype=jnp.int32)[:, None]
    position = position.reshape(4 * cols, slots)
    match = meets(found)
    match = jnp.where((found >= 0)[..., None], match, -1)
    place = jnp.where(jnp.abs(offset) <= HALF, offset + HALF, -1)
    place = jnp.where(place[..., None] >= 0, place[..., None] * cols + q, -1).reshape(-1)
    used = jnp.any(match >= 0, axis=-1)
    turn = position % count // CHUNK
    from_z = position >= 2 * count

    def ready(limits):
        return jnp.all(~used | (turn < jnp.where(from_z, limits[1], limits[0])), axis=1)

    early, usual = ready(EARLY), ready((chunks, ONWARD))
    total_positions = 4 * count

    def step(chosen, parts_held, before):
        sources = [
            (kind * count + k * CHUNK, c) for kind, held in enumerate(parts_held) for k, c in enumerate(held)
        ]
        table = table_of(position, match, jnp.where(chosen, place, -1), total_positions)
        return products(
            slab, table, 4 * cols, slots, total_positions, sources, out_shape, before
        )

    across_other = [permuted(c, partner_core) for c in across]
    along_other = [permuted(c, partner_core) for c in along]
    a, b = EARLY
    held = (across, across_other, along, along_other)
    out = step(usual, held, out)

    late = all_stations % count // CHUNK >= ONWARD
    back = jnp.where(all_chips % 2 == 0, -1, 1)
    readers = all_cols[(all_chips + back) % chips]
    hit = jnp.any(all_rows[:, :, None, None] == readers[:, None], axis=-1)
    of_core = index[:, None] // count - jnp.arange(2)
    within = jnp.abs(of_core - 2 * back[:, None, None]) <= HALF
    rare = jnp.any(hit & within & (late & (all_rows >= 0))[..., None])

    def complete(out):
        more = [permuted(c, onward) for c in across[ONWARD:]]
        more_other = [permuted(c, partner_core) for c in more]
        return step(~usual, (across, across_other, along + more, along_other + more_other), out)

    return lax.cond(rare, complete, lambda out: out, out)


def solution(mesh):
    placed = (
        P(("grp", "blk"), None, None, None, None, None),
        P("blk", None),
        P(("grp", "blk"), None, None, None, None, None),
        P("blk", None),
        P("blk"),
    )
    return jax.shard_map(
        shards,
        mesh=mesh,
        in_specs=placed,
        out_specs=P(("grp", "blk"), None, None, None, None),
        check_vma=False,
    )
```
